32 devices in a mesh: tm: 2 (over core), space: 16 (over z, y, x).
Axes of the slice: x: 2, y: 2, z: 4, core: 2. Of those that a mesh axis runs over, the one named last changes fastest.
Arguments:
- initial: float32 [64, 64, 128], P('space'), may hold values from -6 to 6
- guess: float32 [8, 64, 64, 128], P('tm', 'space'), may hold values from -6 to 6
- conduct: float32 [64, 64, 128], P('space'), may hold values from 0.3 to 3
- source: float32 [64, 64, 128], P('space'), may hold values from -6 to 6
- profile: float32 [64], P('tm'), may hold values from -1 to 1
Outputs:
- corrected: float32 [8, 64, 64, 128], P('tm', 'space')
- residual: float32 [8, 64, 64, 128], P('tm', 'space')
The draws below stay inside these ranges and needn't reach their ends.
All inputs are finite; a program needn't handle non-finite values.
Results may differ from the reference program's by a relative error of at most 0.000048.
Values sent between devices are 32-bit elements; how exact they have to be, the bound alone decides.
No kernel may reach another device: no remote copies, remote signals or barrier semaphores. Data moves between devices by JAX's collectives and lax.ppermute only.
A program may use at most 64 MiB of HBM per device.

```python
import math
import jax
import jax.numpy as jnp

NX = 64
NY = 128
COARSEN = 8
SWEEPS = 3
NZ = 64
INTERVALS = 8
STEPS = 64


def block_levels(own_key, extent, pieces, least, largest):
    level, own = 1.0, jax.random.fold_in(own_key, 6)
    for dim, parts in pieces:
        heights = jnp.exp(jax.random.uniform(jax.random.fold_in(own, dim), (parts,), jnp.float32, least / len(pieces), largest / len(pieces)))
        level = level * jnp.repeat(heights, extent[dim] // parts).reshape([-1 if axis == dim else 1 for axis in range(len(extent))])
    return level


def bell_draw(key, extent, deviation, limit, shards=(), kind=jnp.bfloat16):
    loudness = block_levels(key, extent, shards, -0.22, 0.18) if shards else 1.0
    array = jax.random.normal(key, extent, jnp.float32) * deviation * loudness
    return jnp.minimum(jnp.maximum(array, -limit), limit).astype(kind)


def setup_inputs(seed: int = 0) -> dict:
    splits = jax.random.split(jax.random.key(seed), 6)
    return {
        "initial": bell_draw(splits[0], (NZ, NX, NY), 1.0, 6.0, ((0, 16),), jnp.float32),
        "guess": bell_draw(splits[1], (INTERVALS, NZ, NX, NY), 1.0, 6.0, ((0, 2), (1, 16)), jnp.float32),
        "conduct": jnp.clip(jnp.exp(math.log(3.0) - 2.3025851 * jax.random.uniform(splits[2], (NZ, NX, NY), jnp.float32) ** block_levels(splits[2], (NZ, NX, NY), ((0, 16),), -0.2, 0.2)), 0.3, 3.0),
        "source": bell_draw(splits[3], (NZ, NX, NY), 1.0, 6.0, ((0, 16),), jnp.float32),
        "profile": jnp.clip(jax.random.uniform(splits[4], (STEPS,), jnp.float32, -1.0, 1.0) * block_levels(splits[4], (STEPS,), ((0, 2),), -0.4, 0.0), -1.0, 1.0),
    }


KAPPA_TOP = 3.0


def laplace(field):
    padded = jnp.pad(field, ((0, 0), (1, 1), (1, 1), (1, 1)))
    centre = padded[:, 1:-1, 1:-1, 1:-1]
    beside = padded[:, 2:, 1:-1, 1:-1] + padded[:, :-2, 1:-1, 1:-1]
    beside = beside + padded[:, 1:-1, 2:, 1:-1] + padded[:, 1:-1, :-2, 1:-1]
    beside = beside + padded[:, 1:-1, 1:-1, 2:] + padded[:, 1:-1, 1:-1, :-2]
    return 6.0 * centre - beside


def advance(start, amount, conduct, source, scale, top):
    middle = (top + 1.0) / 2.0
    spread = (top - 1.0) / 2.0
    relative = middle / spread
    ratio_now = 1.0 / relative
    remain = amount * source - scale * conduct * laplace(start)
    update = remain / middle
    iterate = start + update
    for sweep in range(SWEEPS - 1):
        remain = remain - (update + scale * conduct * laplace(update))
        ratio_next = 1.0 / (2.0 * relative - ratio_now)
        update = ratio_next * ratio_now * update + (2.0 * ratio_next / spread) * remain
        iterate = iterate + update
        ratio_now = ratio_next
    return iterate


def reference(initial, guess, conduct, source, profile):
    amounts = profile.reshape(INTERVALS, COARSEN)
    fine_top = 1.0 + 12.0 * KAPPA_TOP
    coarse_top = 1.0 + 12.0 * KAPPA_TOP * COARSEN

    def sweep_interval(entry):
        state = entry
        for inner in range(COARSEN):
            state = advance(state, amounts[:, inner][:, None, None, None], conduct, source, 1.0, fine_top)
        return state

    entry = jnp.concatenate([initial[None], guess[:-1]], axis=0)
    relaxed = sweep_interval(entry)
    again = jnp.concatenate([initial[None], relaxed[:-1]], axis=0)
    residual = sweep_interval(again) - relaxed
    nothing = jnp.zeros((1, 1, 1, 1), jnp.float32)
    error = jnp.zeros_like(initial)
    collected = []
    for section in range(INTERVALS):
        error = advance(error[None], nothing, conduct, source, float(COARSEN), coarse_top)[0] + residual[section]
        collected.append(error)
    corrected = relaxed + jnp.stack(collected, axis=0)
    return corrected, residual
```

```python
from functools import partial

import jax
import jax.numpy as jnp
import numpy as np
from jax import lax
from jax.experimental import pallas as pl
from jax.experimental.pallas import tpu as pltpu
from jax.sharding import PartitionSpec as P

COARSEN = 8
SWEEPS = 3
KAPPA_TOP = 3.0
SUB = 8
PLANES = 16
VMEM = pltpu.CompilerParams(vmem_limit_bytes=48 * 2**20)


def polynomials(scale, top):
    middle = (top + 1.0) / 2.0
    spread = (top - 1.0) / 2.0
    relative = middle / spread

    def run(start, source):
        def apply(poly):
            return scale * np.concatenate([[0.0], poly])[: SWEEPS + 1]

        ratio_now = 1.0 / relative
        remain = source - apply(start)
        update = remain / middle
        iterate = start + update
        for _ in range(SWEEPS - 1):
            remain = remain - (update + apply(update))
            ratio_next = 1.0 / (2.0 * relative - ratio_now)
            update = ratio_next * ratio_now * update + (2.0 * ratio_next / spread) * remain
            iterate = iterate + update
            ratio_now = ratio_next
        return iterate

    one = np.zeros(SWEEPS + 1)
    one[0] = 1.0
    return run(one, 0.0 * one), run(0.0 * one, one)


def linear_factors(poly):
    roots = np.roots(poly[::-1] / poly[-1])
    assert np.all(np.abs(roots.imag) < 1e-9)
    return sorted((float(1.0 / r) for r in roots.real), reverse=True)


FINE_P, FINE_Q = polynomials(1.0, 1.0 + 12.0 * KAPPA_TOP)
COARSE_P, _ = polynomials(float(COARSEN), 1.0 + 12.0 * KAPPA_TOP * COARSEN)
FINE = linear_factors(FINE_P)
COARSE = linear_factors(COARSE_P)


def rows(ref, z, j, J):
    return ref[z, pl.ds(j, SUB, stride=J), :]


def put_rows(ref, z, j, J, value):
    ref[z, pl.ds(j, SUB, stride=J), :] = value


def copy_planes(n, dst, src, d0=0, s0=0):
    J = dst.shape[1]

    def one(z, c):
        for j in range(J):
            dst[d0 + z, j] = src[s0 + z, j]
        return c

    lax.fori_loop(0, n, one, 0, unroll=4 if n % 4 == 0 else 3 if n % 3 == 0 else 1)


def masks(width):
    lane = lax.broadcasted_iota(jnp.int32, (SUB, width), 1)
    sub = lax.broadcasted_iota(jnp.int32, (SUB, width), 0)
    return lane == 0, lane == width - 1, sub == 0, sub == SUB - 1


def sweep(lo, hi, read, emit, J, width):
    first, last, top, bottom = masks(width)
    n = hi - lo
    steps = -(-n // PLANES)
    size = -(-n // steps)

    def chunk(i, c):
        z0 = jnp.minimum(lo + i * size, hi - size)
        for u in range(size):
            z = z0 + u
            w = [read(z, j) for j in range(J)]
            after = jnp.where(bottom, 0.0, pltpu.roll(w[0], SUB - 1, 0))
            before = jnp.where(top, 0.0, pltpu.roll(w[J - 1], 1, 0))
            for j in range(J):
                yp = w[j + 1] if j < J - 1 else after
                ym = w[j - 1] if j > 0 else before
                xm = jnp.where(first, 0.0, pltpu.roll(w[j], 1, 1))
                xp = jnp.where(last, 0.0, pltpu.roll(w[j], width - 1, 1))
                beside = (read(z - 1, j) + read(z + 1, j)) + (yp + ym) + (xm + xp)
                emit(z, j, w[j], beside)
        return c

    lax.fori_loop(0, steps, chunk, 0)


def factor(dst, src, cond, coef, lo, hi, s0=0, k0=0, extra=None):
    J, width = dst.shape[1], dst.shape[3]

    def emit(z, j, w, beside):
        out = w + (coef * cond[z + k0, j]) * (beside - 6.0 * w)
        if extra is not None:
            out = out + extra(z, j)
        dst[z, j] = out

    sweep(lo, hi, lambda z, j: src[z + s0, j], emit, J, width)


def fine_steps(a, b, cond, k0, total, levels, amounts=None, first_step=0, source=None):
    src, dst = a, b
    for level in range(levels):
        extra = None
        if source is not None and level % SWEEPS == SWEEPS - 1:
            amount = amounts[first_step + level // SWEEPS]
            extra = lambda z, j, amount=amount: amount * source[z + k0, j]
        factor(dst, src, cond, FINE[level % SWEEPS], level + 1, total - level - 1, k0=k0, extra=extra)
        src, dst = dst, src
    return src


def place_kernel(where, own, r1, r2, r3, field, coef, field_up, field_dn, *, each, halo, wide):
    q = where[0]
    J = field.shape[1]
    for j, ref in enumerate((own, r1, r2, r3)):
        base = lax.bitwise_xor(q, j) * each
        for z in range(each):
            for row in range(J):
                field[base + z, row] = rows(ref, z, row, J)
                coef[base + z, row] = rows(ref, each + z, row, J)
    slab = field.shape[0]
    copy_planes(halo, field_up, field, 0, slab - halo)
    copy_planes(wide, field_up, coef, halo, slab - wide)
    copy_planes(halo, field_dn, field, 0, 0)
    copy_planes(wide, field_dn, coef, halo, 0)


def first_kernel(
    where, amounts, field, mine, other, got_lo, got_hi, other_lo, other_hi,
    out, up, dn, cond, force, a, b, raw, *, halo, wide,
):
    core = where[1]
    J, width = a.shape[1], a.shape[3]
    slab = field.shape[0]
    total = slab + 2 * halo
    span = slab + 2 * wide
    copy_planes(halo, a, got_lo, 0, 0)
    copy_planes(slab, a, field, halo, 0)
    copy_planes(halo, a, got_hi, halo + slab, 0)

    def fill(slot, lo, mid, hi, off):
        def one(n, src, d0, s0):
            def body(z, c):
                for j in range(J):
                    raw[slot, d0 + z, j] = src[s0 + z, j]
                return c

            lax.fori_loop(0, n, body, 0)

        one(wide, lo, 0, off)
        one(slab, mid, wide, 0)
        one(wide, hi, wide + slab, off)

    fill(core, got_lo, mine, got_hi, halo)
    fill(1 - core, other_lo, other, other_hi, 0)
    copy_planes(span, cond, raw.at[0])

    def inner(z, j, w, beside):
        raw[0, z, j] = FINE_Q[1] * w + FINE_Q[2] * cond[z, j] * (6.0 * w - beside)

    def outer(z, j, w, beside):
        force[z, j] = FINE_Q[0] * raw[1, z, j] + cond[z, j] * (6.0 * w - beside)

    margin = wide - (halo - SWEEPS)
    sweep(margin - 1, span - margin + 1, lambda z, j: raw[1, z, j], inner, J, width)
    sweep(margin, span - margin, lambda z, j: raw[0, z, j], outer, J, width)

    state = fine_steps(a, b, cond, wide - halo, total, halo, amounts, 0, force)
    copy_planes(slab, out, state, 0, halo)
    copy_planes(halo, up, state, 0, halo + slab - halo)
    copy_planes(halo, dn, state, 0, halo)


def load_state(a, lo, mid, hi):
    halo, slab = lo.shape[0], mid.shape[0]
    copy_planes(halo, a, lo, 0, 0)
    copy_planes(slab, a, mid, halo, 0)
    copy_planes(halo, a, hi, halo + slab, 0)


def second_kernel(
    where, amounts, field, lo, hi, cond, force, n0, n1, n2, n3,
    p0, p1, p2, p3, out, up, dn, a, b, *, wide, each, step,
):
    q = where[0]
    halo, slab, J = lo.shape[0], field.shape[0], a.shape[1]
    load_state(a, lo, field, hi)
    state = fine_steps(a, b, cond, wide - halo, slab + 2 * halo, halo, amounts, step, force)
    for i, (piece, after) in enumerate(((p0, n0), (p1, n1), (p2, n2), (p3, n3))):
        base = lax.bitwise_xor(q, i) * each
        for z in range(each):
            for j in range(J):
                value = state[halo + base + z, j]
                put_rows(piece, z, j, J, value)
                out[base + z, j] = value - rows(after, z, j, J)
    copy_planes(halo, up, out, 0, slab - halo)
    copy_planes(halo, dn, out, 0, 0)


def third_kernel(field, lo, hi, cond, out, up, dn, a, b, *, wide):
    halo, slab = lo.shape[0], field.shape[0]
    load_state(a, lo, field, hi)
    state = fine_steps(a, b, cond, wide - halo, slab + 2 * halo, halo)
    copy_planes(slab, out, state, 0, halo)
    copy_planes(up.shape[0], up, state, 0, halo + slab - up.shape[0])
    copy_planes(dn.shape[0], dn, state, 0, halo)


def fourth_kernel(where, field, lo, hi, cond, out, p0, p1, p2, p3, a, b, *, levels, each):
    q = where[0]
    halo, slab, J = lo.shape[0], field.shape[0], a.shape[1]
    load_state(a, lo, field, hi)
    state = fine_steps(a, b, cond, 0, slab + 2 * halo, levels)
    copy_planes(out.shape[0], out, state, 0, levels)
    for i, piece in enumerate((p0, p1, p2, p3)):
        base = lax.bitwise_xor(q, i) * each
        for z in range(each):
            for j in range(J):
                put_rows(piece, z, j, J, state[halo + base + z, j])


def pair_kernel(where, mine, other, cond, out, both, a, b, *, wide):
    core = where[1]
    J = a.shape[1]
    total = mine.shape[0]
    slab = out.shape[0]

    def body(z, c):
        for j in range(J):
            both[core, z, j] = mine[z, j]
            both[1 - core, z, j] = other[z, j]
        return c

    lax.fori_loop(0, total, body, 0)
    k0 = wide - SWEEPS
    factor(a, both.at[0], cond, COARSE[0], 1, total - 1, k0=k0)
    factor(b, a, cond, COARSE[1], 2, total - 2, k0=k0)
    factor(a, b, cond, COARSE[2], 3, total - 3, k0=k0, extra=lambda z, j: both[1, z, j])
    copy_planes(slab, out, a, 0, SWEEPS)


def chain_kernel(where, sums, got_lo, got_hi, cond, *refs, wide, each, reach):
    pieces, refs = refs[:16], refs[16:]
    corrected, residual, ends, a, b, c, d, relaxed, remain, error = refs
    q, core = where[0], where[1]
    J = a.shape[1]
    count = len(reach) + 1
    slab = sums.shape[0] // count
    mine_rel, other_rel, mine_res, other_res = (pieces[4 * i : 4 * i + 4] for i in range(4))
    for i in range(4):
        place = lax.bitwise_xor(q, i)
        for z in range(each):
            for j in range(J):
                relaxed[2 * place + core, z, j] = rows(mine_rel[i], z, j, J)
                relaxed[2 * place + 1 - core, z, j] = rows(other_rel[i], z, j, J)
                remain[2 * place + 1 + core, z, j] = rows(mine_res[i], z, j, J)
                remain[2 * place + 2 - core, z, j] = rows(other_res[i], z, j, J)
    zero = jnp.zeros(a.shape[2:], jnp.float32)
    for z in range(each):
        for j in range(J):
            remain[0, z, j] = zero
            error[0, z, j] = zero
    offset = 0
    for i, h in enumerate(reach):
        copy_planes(h, ends.at[i], got_lo, 0, offset)
        copy_planes(slab, ends.at[i], sums, h, i * slab)
        copy_planes(h, ends.at[i], got_hi, h + slab, offset)
        offset += h
    top = reach[0]
    window = each + 2 * top
    base = each * q

    def keep(k, ref, s0):
        for z in range(each):
            for j in range(J):
                error[k, z, j] = ref[top + z + s0, j]

    keep(2, ends.at[0], base)
    for z in range(each):
        for j in range(J):
            error[1, z, j] = remain[1, z, j]
    src, s0, lo, hi = ends.at[0], base, 0, window
    for i in range(len(reach)):
        k = 2 * i + 3
        inner = dict(k0=base)
        m0, m1 = top, top + each
        factor(c, src, cond, COARSE[0], m0 - 2, m1 + 2, s0=s0, **inner)
        factor(d, c, cond, COARSE[1], m0 - 1, m1 + 1, **inner)
        factor(c, d, cond, COARSE[2], m0, m1, extra=lambda z, j, k=k: remain[k, z - top, j], **inner)
        keep(k, c, 0)
        if i + 1 < len(reach):
            nxt = ends.at[i + 1]
            shift = base - top + reach[i + 1]
            bufs = (a, b)
            for level in range(2 * SWEEPS):
                lo, hi = lo + 1, hi - 1
                dst = bufs[level % 2]
                extra = None
                if level == 2 * SWEEPS - 1:
                    extra = lambda z, j, nxt=nxt, shift=shift: nxt[z + shift, j]
                factor(dst, src, cond, COARSE[level % SWEEPS], lo, hi, s0=s0, extra=extra, **inner)
                src, s0 = dst, 0
            keep(2 * i + 4, src, 0)
    slots = corrected.shape[0]
    for i in range(slots):
        k = core * slots + i
        for z in range(each):
            for j in range(J):
                corrected[i, z, pl.ds(j, SUB, stride=J), :] = relaxed[k, z, j] + error[k, z, j]
                residual[i, z, pl.ds(j, SUB, stride=J), :] = remain[k, z, j]


def body(initial, guess, conduct, source, profile):
    slots, each, nx, ny = guess.shape
    J = nx // SUB
    cores = lax.axis_size("tm")
    count = lax.axis_size("space")
    assert cores == 2 and slots == 4 and count % slots == 0 and nx % SUB == 0
    core = lax.axis_index("tm")
    place = lax.axis_index("space")
    q = place % slots
    slab = slots * each
    halo = COARSEN * SWEEPS // 2
    wide = halo + SWEEPS
    where = jnp.stack([q, core]).astype(jnp.int32)
    f32 = jnp.float32

    def blocked(n):
        return jax.ShapeDtypeStruct((n, J, SUB, ny), f32)

    def natural(n):
        return jax.ShapeDtypeStruct((n, nx, ny), f32)

    def scratch(*lead):
        return pltpu.VMEM((*lead, J, SUB, ny), f32)

    smem = pl.BlockSpec(memory_space=pltpu.SMEM)
    vmem = pl.BlockSpec(memory_space=pltpu.VMEM)

    def call(kernel, scalars, arrays, outs, scratches, name):
        return pl.pallas_call(
            kernel,
            out_shape=outs,
            in_specs=[smem] * len(scalars) + [vmem] * len(arrays),
            out_specs=jax.tree.map(lambda _: vmem, outs),
            scratch_shapes=scratches,
            compiler_params=VMEM,
            name=name,
        )(*scalars, *arrays)

    def swap(value):
        return lax.ppermute(value, "tm", [(0, 1), (1, 0)])

    def across(value, j):
        return lax.ppermute(value, "space", [(s, s - s % slots + ((s % slots) ^ j)) for s in range(count)])

    def up(value):
        return lax.ppermute(value, "space", [(s, s + slots) for s in range(count - slots)])

    def down(value):
        return lax.ppermute(value, "space", [(s + slots, s) for s in range(count - slots)])

    first = core == 0
    theirs = swap(guess)
    low, high = jnp.where(first, guess, theirs), jnp.where(first, theirs, guess)
    guesses = jnp.concatenate([low, high], axis=0)
    amounts_other = swap(profile)
    profiles = jnp.concatenate([jnp.where(first, profile, amounts_other), jnp.where(first, amounts_other, profile)])
    task = 2 * q + core
    amounts = lax.dynamic_slice_in_dim(profiles, task * COARSEN, COARSEN)

    entries = jnp.concatenate([initial[None], guesses[:-1]], axis=0)
    coef = jnp.where(first, conduct, source)

    def entry_for(j):
        t = 2 * (q ^ j) + core
        return jnp.concatenate([lax.dynamic_index_in_dim(entries, t, 0, False), coef], axis=0)

    def after_for(j):
        t = 2 * (q ^ j) + core
        return lax.dynamic_index_in_dim(guesses, t, 0, False)

    got = [entry_for(0)] + [across(entry_for(j), j) for j in range(1, slots)]
    after = [after_for(0)] + [across(after_for(j), j) for j in range(1, slots)]

    field, mine, send_up, send_dn = call(
        partial(place_kernel, each=each, halo=halo, wide=wide),
        [where], got, [blocked(slab), blocked(slab), blocked(halo + wide), blocked(halo + wide)], [], "place",
    )
    other = swap(mine)
    got_lo, got_hi = up(send_up), down(send_dn)
    other_lo, other_hi = swap(got_lo[halo:]), swap(got_hi[halo:])
    span, total = slab + 2 * wide, slab + 2 * halo
    state, send_up, send_dn, cond, force = call(
        partial(first_kernel, halo=halo, wide=wide),
        [where, amounts], [field, mine, other, got_lo, got_hi, other_lo, other_hi],
        [blocked(slab), blocked(halo), blocked(halo), blocked(span), blocked(span)],
        [scratch(total), scratch(total), scratch(2, span)], "relax_first",
    )
    *rel, state, send_up, send_dn = call(
        partial(second_kernel, wide=wide, each=each, step=halo // SWEEPS),
        [where, amounts], [state, up(send_up), down(send_dn), cond, force, *after],
        [natural(each)] * 4 + [blocked(slab), blocked(halo), blocked(halo)],
        [scratch(total), scratch(total)], "relax_second",
    )
    rel = [rel[0]] + [across(rel[j], j) for j in range(1, slots)]
    state, send_up, send_dn = call(
        partial(third_kernel, wide=wide),
        [], [state, up(send_up), down(send_dn), cond],
        [blocked(slab), blocked(wide), blocked(wide)],
        [scratch(total), scratch(total)], "again_first",
    )
    remain, *res = call(
        partial(fourth_kernel, levels=halo, each=each),
        [where], [state, up(send_up), down(send_dn), cond],
        [blocked(slab + 2 * SWEEPS)] + [natural(each)] * 4,
        [scratch(span), scratch(span)], "again_second",
    )
    res = [res[0]] + [across(res[j], j) for j in range(1, slots)]
    rel_other = [swap(r) for r in rel]
    res_other = [swap(r) for r in res]

    pair = call(
        partial(pair_kernel, wide=wide),
        [where], [remain, swap(remain), cond],
        blocked(slab), [scratch(2, slab + 2 * SWEEPS), scratch(slab + 2 * SWEEPS), scratch(slab + 2 * SWEEPS)], "pairs",
    )
    groups = [[g * slots + i for i in range(slots)] for g in range(count // slots)]
    sums = lax.all_gather(pair, "space", axis=0, tiled=True, axis_index_groups=groups)
    reach = [2 * SWEEPS * (slots - 2 - i) + SWEEPS for i in range(slots - 1)]
    send_up = jnp.concatenate([sums[(i + 1) * slab - h : (i + 1) * slab] for i, h in enumerate(reach)], axis=0)
    send_dn = jnp.concatenate([sums[i * slab : i * slab + h] for i, h in enumerate(reach)], axis=0)
    window = each + 2 * reach[0]
    corrected, residual = call(
        partial(chain_kernel, wide=wide, each=each, reach=reach),
        [where], [sums, up(send_up), down(send_dn), cond, *rel, *rel_other, *res, *res_other],
        [jax.ShapeDtypeStruct(guess.shape, f32)] * 2,
        [scratch(len(reach), slab + 2 * reach[0])]
        + [scratch(window)] * 4
        + [scratch(2 * slots, each), scratch(2 * slots + 1, each), scratch(2 * slots, each)],
        "chain",
    )
    return corrected, residual


def solution(mesh):
    return jax.shard_map(
        body,
        mesh=mesh,
        in_specs=(
            P("space", None, None),
            P("tm", "space", None, None),
            P("space", None, None),
            P("space", None, None),
            P("tm"),
        ),
        out_specs=(P("tm", "space", None, None), P("tm", "space", None, None)),
        check_vma=False,
    )
```

```python
from functools import partial

import jax
import jax.numpy as jnp
import numpy as np
from jax import lax
from jax.experimental import pallas as pl
from jax.experimental.pallas import tpu as pltpu
from jax.sharding import PartitionSpec as P

COARSEN = 8
SWEEPS = 3
KAPPA_TOP = 3.0
SUB = 8
PLANES = 16
VMEM = pltpu.CompilerParams(vmem_limit_bytes=48 * 2**20)


def polynomials(scale, top):
    middle = (top + 1.0) / 2.0
    spread = (top - 1.0) / 2.0
    relative = middle / spread

    def run(start, source):
        def apply(poly):
            return scale * np.concatenate([[0.0], poly])[: SWEEPS + 1]

        ratio_now = 1.0 / relative
        remain = source - apply(start)
        update = remain / middle
        iterate = start + update
        for _ in range(SWEEPS - 1):
            remain = remain - (update + apply(update))
            ratio_next = 1.0 / (2.0 * relative - ratio_now)
            update = ratio_next * ratio_now * update + (2.0 * ratio_next / spread) * remain
            iterate = iterate + update
            ratio_now = ratio_next
        return iterate

    one = np.zeros(SWEEPS + 1)
    one[0] = 1.0
    return run(one, 0.0 * one), run(0.0 * one, one)


def linear_factors(poly):
    roots = np.roots(poly[::-1] / poly[-1])
    assert np.all(np.abs(roots.imag) < 1e-9)
    return sorted((float(1.0 / r) for r in roots.real), reverse=True)


FINE_P, FINE_Q = polynomials(1.0, 1.0 + 12.0 * KAPPA_TOP)
COARSE_P, _ = polynomials(float(COARSEN), 1.0 + 12.0 * KAPPA_TOP * COARSEN)
FINE = linear_factors(FINE_P)
COARSE = linear_factors(COARSE_P)


def rows(ref, z, j, J):
    return ref[z, pl.ds(j, SUB, stride=J), :]


def put_rows(ref, z, j, J, value):
    ref[z, pl.ds(j, SUB, stride=J), :] = value


def copy_planes(n, dst, src, d0=0, s0=0):
    J = dst.shape[1]

    def one(z, c):
        for j in range(J):
            dst[d0 + z, j] = src[s0 + z, j]
        return c

    lax.fori_loop(0, n, one, 0, unroll=4 if n % 4 == 0 else 3 if n % 3 == 0 else 1)


def masks(width):
    lane = lax.broadcasted_iota(jnp.int32, (SUB, width), 1)
    sub = lax.broadcasted_iota(jnp.int32, (SUB, width), 0)
    return lane == 0, lane == width - 1, sub == 0, sub == SUB - 1


def sweep(lo, hi, read, emit, J, width):
    first, last, top, bottom = masks(width)
    n = hi - lo
    steps = -(-n // PLANES)
    size = -(-n // steps)

    def chunk(i, c):
        z0 = jnp.minimum(lo + i * size, hi - size)
        for u in range(size):
            z = z0 + u
            w = [read(z, j) for j in range(J)]
            after = jnp.where(bottom, 0.0, pltpu.roll(w[0], SUB - 1, 0))
            before = jnp.where(top, 0.0, pltpu.roll(w[J - 1], 1, 0))
            for j in range(J):
                yp = w[j + 1] if j < J - 1 else after
                ym = w[j - 1] if j > 0 else before
                xm = jnp.where(first, 0.0, pltpu.roll(w[j], 1, 1))
                xp = jnp.where(last, 0.0, pltpu.roll(w[j], width - 1, 1))
                beside = (read(z - 1, j) + read(z + 1, j)) + (yp + ym) + (xm + xp)
                emit(z, j, w[j], beside)
        return c

    lax.fori_loop(0, steps, chunk, 0)


def factor(dst, src, cond, coef, lo, hi, s0=0, k0=0, extra=None):
    J, width = dst.shape[1], dst.shape[3]

    def emit(z, j, w, beside):
        out = w + (coef * cond[z + k0, j]) * (beside - 6.0 * w)
        if extra is not None:
            out = out + extra(z, j)
        dst[z, j] = out

    sweep(lo, hi, lambda z, j: src[z + s0, j], emit, J, width)


def fine_steps(a, b, cond, k0, total, levels, amounts=None, first_step=0, source=None):
    src, dst = a, b
    for level in range(levels):
        extra = None
        if source is not None and level % SWEEPS == SWEEPS - 1:
            amount = amounts[first_step + level // SWEEPS]
            extra = lambda z, j, amount=amount: amount * source[z + k0, j]
        factor(dst, src, cond, FINE[level % SWEEPS], level + 1, total - level - 1, k0=k0, extra=extra)
        src, dst = dst, src
    return src


def place_kernel(where, own, r1, r2, r3, field, field_up, field_dn, *, each):
    q = where[0]
    J = field.shape[1]
    for j, ref in enumerate((own, r1, r2, r3)):
        base = lax.bitwise_xor(q, j) * each
        for z in range(each):
            for row in range(J):
                field[base + z, row] = rows(ref, z, row, J)
    halo = field_up.shape[0]
    copy_planes(halo, field_up, field, 0, field.shape[0] - halo)
    copy_planes(halo, field_dn, field, 0, 0)


def first_kernel(
    where, amounts, field, lo, hi, m0, m1, m2, m3, o0, o1, o2, o3,
    out, up, dn, cond, force, a, b, raw, *, wide, each,
):
    q, core = where[0], where[1]
    J, width = a.shape[1], a.shape[3]
    slab, halo = field.shape[0], lo.shape[0]
    total = slab + 2 * halo
    span = slab + 2 * wide
    load_state(a, lo, field, hi)
    skip = slab - wide
    for i, pieces in enumerate(zip((m0, m1, m2, m3), (o0, o1, o2, o3))):
        base = lax.bitwise_xor(q, i) * each
        for slot, ref in zip((core, 1 - core), pieces):
            for part in range(3):
                for z in range(each):
                    for j in range(J):
                        raw[slot, part * slab + base + z, j] = rows(ref, part * each + z, j, J)
    copy_planes(span, cond, raw.at[0], 0, skip)

    def inner(z, j, w, beside):
        raw[0, z + skip, j] = FINE_Q[1] * w + FINE_Q[2] * cond[z, j] * (6.0 * w - beside)

    def outer(z, j, w, beside):
        force[z, j] = FINE_Q[0] * raw[1, z + skip, j] + cond[z, j] * (6.0 * w - beside)

    margin = wide - (halo - SWEEPS)
    sweep(margin - 1, span - margin + 1, lambda z, j: raw[1, z + skip, j], inner, J, width)
    sweep(margin, span - margin, lambda z, j: raw[0, z + skip, j], outer, J, width)

    state = fine_steps(a, b, cond, wide - halo, total, halo, amounts, 0, force)
    copy_planes(slab, out, state, 0, halo)
    copy_planes(halo, up, state, 0, halo + slab - halo)
    copy_planes(halo, dn, state, 0, halo)


def load_state(a, lo, mid, hi):
    halo, slab = lo.shape[0], mid.shape[0]
    copy_planes(halo, a, lo, 0, 0)
    copy_planes(slab, a, mid, halo, 0)
    copy_planes(halo, a, hi, halo + slab, 0)


def second_kernel(
    where, amounts, field, lo, hi, cond, force, n0, n1, n2, n3,
    p0, p1, p2, p3, out, up, dn, a, b, *, wide, each, step,
):
    q = where[0]
    halo, slab, J = lo.shape[0], field.shape[0], a.shape[1]
    load_state(a, lo, field, hi)
    state = fine_steps(a, b, cond, wide - halo, slab + 2 * halo, halo, amounts, step, force)
    for i, (piece, after) in enumerate(((p0, n0), (p1, n1), (p2, n2), (p3, n3))):
        base = lax.bitwise_xor(q, i) * each
        for z in range(each):
            for j in range(J):
                value = state[halo + base + z, j]
                put_rows(piece, z, j, J, value)
                out[base + z, j] = value - rows(after, z, j, J)
    copy_planes(halo, up, out, 0, slab - halo)
    copy_planes(halo, dn, out, 0, 0)


def third_kernel(field, lo, hi, cond, out, up, dn, a, b, *, wide):
    halo, slab = lo.shape[0], field.shape[0]
    load_state(a, lo, field, hi)
    state = fine_steps(a, b, cond, wide - halo, slab + 2 * halo, halo)
    copy_planes(slab, out, state, 0, halo)
    copy_planes(up.shape[0], up, state, 0, halo + slab - up.shape[0])
    copy_planes(dn.shape[0], dn, state, 0, halo)


def fourth_kernel(where, field, lo, hi, cond, out, p0, p1, p2, p3, a, b, *, levels, each):
    q = where[0]
    halo, slab, J = lo.shape[0], field.shape[0], a.shape[1]
    load_state(a, lo, field, hi)
    state = fine_steps(a, b, cond, 0, slab + 2 * halo, levels)
    copy_planes(out.shape[0], out, state, 0, levels)
    for i, piece in enumerate((p0, p1, p2, p3)):
        base = lax.bitwise_xor(q, i) * each
        for z in range(each):
            for j in range(J):
                put_rows(piece, z, j, J, state[halo + base + z, j])


def pair_kernel(where, mine, other, cond, out, both, a, b, *, wide):
    core = where[1]
    J = a.shape[1]
    total = mine.shape[0]
    slab = out.shape[0]

    def body(z, c):
        for j in range(J):
            both[core, z, j] = mine[z, j]
            both[1 - core, z, j] = other[z, j]
        return c

    lax.fori_loop(0, total, body, 0)
    k0 = wide - SWEEPS
    factor(a, both.at[0], cond, COARSE[0], 1, total - 1, k0=k0)
    factor(b, a, cond, COARSE[1], 2, total - 2, k0=k0)
    factor(a, b, cond, COARSE[2], 3, total - 3, k0=k0, extra=lambda z, j: both[1, z, j])
    half = out.shape[1]

    def give(z, c):
        for j in range(half):
            out[z, j] = a[SWEEPS + z, core * half + j]
        return c

    lax.fori_loop(0, slab, give, 0)


def order_kernel(where, own, r1, r2, r3, sums, send_up, send_dn, all_sums, *, reach):
    q = where[0]
    slab = own.shape[0]
    for i, ref in enumerate((own, r1, r2, r3)):
        copy_planes(slab, all_sums, ref, lax.bitwise_xor(q, i) * slab, 0)
    offset = 0
    for i, h in enumerate(reach):
        copy_planes(slab, sums, all_sums, i * slab, i * slab)
        copy_planes(h, send_up, all_sums, offset, (i + 1) * slab - h)
        copy_planes(h, send_dn, all_sums, offset, i * slab)
        offset += h


def chain_kernel(
    where, sums, got_lo, got_hi, other_sums, other_lo, other_hi, cond, *refs, wide, each, reach
):
    pieces, refs = refs[:10], refs[10:]
    corrected, residual, ends, a, b, c, d, relaxed, remain, error = refs
    q, core = where[0], where[1]
    J = a.shape[1]
    slab = sums.shape[0] // len(reach)
    half = J // 2
    mine_rel, other_rel, mine_res, other_res = pieces[:4], pieces[4], pieces[5:9], pieces[9]
    for i in range(4):
        place = lax.bitwise_xor(q, i)
        for z in range(each):
            for j in range(J):
                relaxed[2 * place + core, z, j] = rows(mine_rel[i], z, j, J)
                relaxed[2 * place + 1 - core, z, j] = rows(other_rel, i * each + z, j, J)
                remain[2 * place + 1 + core, z, j] = rows(mine_res[i], z, j, J)
                remain[2 * place + 2 - core, z, j] = rows(other_res, i * each + z, j, J)
    zero = jnp.zeros(a.shape[2:], jnp.float32)
    for z in range(each):
        for j in range(J):
            remain[0, z, j] = zero
            error[0, z, j] = zero
    offset = 0
    for i, h in enumerate(reach):

        def fill(n, mine, other, d0, s0, i=i):
            def one(z, carry):
                for j in range(half):
                    ends[i, d0 + z, core * half + j] = mine[s0 + z, j]
                    ends[i, d0 + z, (1 - core) * half + j] = other[s0 + z, j]
                return carry

            lax.fori_loop(0, n, one, 0)

        fill(h, got_lo, other_lo, 0, offset)
        fill(slab, sums, other_sums, h, i * slab)
        fill(h, got_hi, other_hi, h + slab, offset)
        offset += h
    top = reach[0]
    window = each + 2 * top
    base = each * q

    def keep(k, ref, s0):
        for z in range(each):
            for j in range(J):
                error[k, z, j] = ref[top + z + s0, j]

    keep(2, ends.at[0], base)
    for z in range(each):
        for j in range(J):
            error[1, z, j] = remain[1, z, j]
    src, s0, lo, hi = ends.at[0], base, 0, window
    for i in range(len(reach)):
        k = 2 * i + 3
        inner = dict(k0=base)
        m0, m1 = top, top + each
        factor(c, src, cond, COARSE[0], m0 - 2, m1 + 2, s0=s0, **inner)
        factor(d, c, cond, COARSE[1], m0 - 1, m1 + 1, **inner)
        factor(c, d, cond, COARSE[2], m0, m1, extra=lambda z, j, k=k: remain[k, z - top, j], **inner)
        keep(k, c, 0)
        if i + 1 < len(reach):
            nxt = ends.at[i + 1]
            shift = base - top + reach[i + 1]
            bufs = (a, b)
            for level in range(2 * SWEEPS):
                lo, hi = lo + 1, hi - 1
                dst = bufs[level % 2]
                extra = None
                if level == 2 * SWEEPS - 1:
                    extra = lambda z, j, nxt=nxt, shift=shift: nxt[z + shift, j]
                factor(dst, src, cond, COARSE[level % SWEEPS], lo, hi, s0=s0, extra=extra, **inner)
                src, s0 = dst, 0
            keep(2 * i + 4, src, 0)
    slots = corrected.shape[0]
    for i in range(slots):
        k = core * slots + i
        for z in range(each):
            for j in range(J):
                corrected[i, z, pl.ds(j, SUB, stride=J), :] = relaxed[k, z, j] + error[k, z, j]
                residual[i, z, pl.ds(j, SUB, stride=J), :] = remain[k, z, j]


def body(initial, guess, conduct, source, profile):
    slots, each, nx, ny = guess.shape
    J = nx // SUB
    cores = lax.axis_size("tm")
    count = lax.axis_size("space")
    assert cores == 2 and slots == 4 and count % slots == 0 and nx % SUB == 0
    core = lax.axis_index("tm")
    place = lax.axis_index("space")
    q = place % slots
    slab = slots * each
    halo = COARSEN * SWEEPS // 2
    wide = halo + SWEEPS
    where = jnp.stack([q, core]).astype(jnp.int32)
    f32 = jnp.float32

    def blocked(n):
        return jax.ShapeDtypeStruct((n, J, SUB, ny), f32)

    def natural(n):
        return jax.ShapeDtypeStruct((n, nx, ny), f32)

    def scratch(*lead):
        return pltpu.VMEM((*lead, J, SUB, ny), f32)

    smem = pl.BlockSpec(memory_space=pltpu.SMEM)
    vmem = pl.BlockSpec(memory_space=pltpu.VMEM)

    def call(kernel, scalars, arrays, outs, scratches, name, micros):
        return pl.pallas_call(
            kernel,
            out_shape=outs,
            in_specs=[smem] * len(scalars) + [vmem] * len(arrays),
            out_specs=jax.tree.map(lambda _: vmem, outs),
            scratch_shapes=scratches,
            compiler_params=VMEM,
            cost_estimate=pl.CostEstimate(
                flops=micros * 10**9, bytes_accessed=micros * 3 * 10**6, transcendentals=0
            ),
            name=name,
        )(*scalars, *arrays)

    def swap(value):
        return lax.ppermute(value, "tm", [(0, 1), (1, 0)])

    def across(value, j):
        return lax.ppermute(value, "space", [(s, s - s % slots + ((s % slots) ^ j)) for s in range(count)])

    def up(value):
        return lax.ppermute(value, "space", [(s, s + slots) for s in range(count - slots)])

    def down(value):
        return lax.ppermute(value, "space", [(s + slots, s) for s in range(count - slots)])

    first = core == 0
    theirs = swap(guess)
    low, high = jnp.where(first, guess, theirs), jnp.where(first, theirs, guess)
    guesses = jnp.concatenate([low, high], axis=0)
    amounts_other = swap(profile)
    profiles = jnp.concatenate([jnp.where(first, profile, amounts_other), jnp.where(first, amounts_other, profile)])
    task = 2 * q + core
    amounts = lax.dynamic_slice_in_dim(profiles, task * COARSEN, COARSEN)

    entries = jnp.concatenate([initial[None], guesses[:-1]], axis=0)
    coef = jnp.where(first, conduct, source)
    coef = jnp.concatenate([up(coef), coef, down(coef)], axis=0)

    def entry_for(j):
        return lax.dynamic_index_in_dim(entries, 2 * (q ^ j) + core, 0, False)

    def after_for(j):
        return lax.dynamic_index_in_dim(guesses, 2 * (q ^ j) + core, 0, False)

    def gathered(pieces):
        return [pieces[0]] + [across(pieces[j], j) for j in range(1, slots)]

    field, send_up, send_dn = call(
        partial(place_kernel, each=each),
        [where], gathered([entry_for(j) for j in range(slots)]),
        [blocked(slab), blocked(halo), blocked(halo)], [], "place", 1,
    )
    mine = gathered([coef] * slots)
    lo, hi = up(send_up), down(send_dn)
    span, total = slab + 2 * wide, slab + 2 * halo
    others = [swap(m) for m in mine]
    after = [after_for(j) for j in range(slots)]
    *after, lo = lax.optimization_barrier((*after, lo))
    after = gathered(after)
    state, send_up, send_dn, cond, force = call(
        partial(first_kernel, wide=wide, each=each),
        [where, amounts], [field, lo, hi, *mine, *others],
        [blocked(slab), blocked(halo), blocked(halo), blocked(span), blocked(span)],
        [scratch(total), scratch(total), scratch(2, 3 * slab)], "relax_first", 12,
    )
    *after, send_up, send_dn = lax.optimization_barrier((*after, send_up, send_dn))
    *rel, state, send_up, send_dn = call(
        partial(second_kernel, wide=wide, each=each, step=halo // SWEEPS),
        [where, amounts], [state, up(send_up), down(send_dn), cond, force, *after],
        [natural(each)] * 4 + [blocked(slab), blocked(halo), blocked(halo)],
        [scratch(total), scratch(total)], "relax_second", 9,
    )
    lo, hi = up(send_up), down(send_dn)
    *rel, lo = lax.optimization_barrier((*rel, lo))
    rel = gathered(rel)
    state, send_up, send_dn = call(
        partial(third_kernel, wide=wide),
        [], [state, lo, hi, cond],
        [blocked(slab), blocked(wide), blocked(wide)],
        [scratch(total), scratch(total)], "again_first", 8,
    )
    *rel, send_up, send_dn = lax.optimization_barrier((*rel, send_up, send_dn))
    rel_other = swap(jnp.concatenate(rel, axis=0))
    lo, hi = up(send_up), down(send_dn)
    rel_other, lo = lax.optimization_barrier((rel_other, lo))
    remain, *res = call(
        partial(fourth_kernel, levels=halo, each=each),
        [where], [state, lo, hi, cond],
        [blocked(slab + 2 * SWEEPS)] + [natural(each)] * 4,
        [scratch(span), scratch(span)], "again_second", 9,
    )
    pair = call(
        partial(pair_kernel, wide=wide),
        [where], [remain, swap(remain), cond],
        jax.ShapeDtypeStruct((slab, J // 2, SUB, ny), f32),
        [scratch(2, slab + 2 * SWEEPS), scratch(slab + 2 * SWEEPS), scratch(slab + 2 * SWEEPS)], "pairs", 3,
    )
    reach = [2 * SWEEPS * (slots - 2 - i) + SWEEPS for i in range(slots - 1)]
    halves = lambda n: jax.ShapeDtypeStruct((n, J // 2, SUB, ny), f32)
    sums, send_up, send_dn = call(
        partial(order_kernel, reach=reach),
        [where], gathered([pair] * slots),
        [halves(len(reach) * slab), halves(sum(reach)), halves(sum(reach))],
        [pltpu.VMEM((slots * slab, J // 2, SUB, ny), f32)], "order", 1,
    )
    *res, sums = lax.optimization_barrier((*res, sums))
    res = gathered(res)
    res_other = swap(jnp.concatenate(res, axis=0))
    lo, hi = up(send_up), down(send_dn)
    window = each + 2 * reach[0]
    corrected, residual = call(
        partial(chain_kernel, wide=wide, each=each, reach=reach),
        [where], [sums, lo, hi, swap(sums), swap(lo), swap(hi), cond, *rel, rel_other, *res, res_other],
        [jax.ShapeDtypeStruct(guess.shape, f32)] * 2,
        [scratch(len(reach), slab + 2 * reach[0])]
        + [scratch(window)] * 4
        + [scratch(2 * slots, each), scratch(2 * slots + 1, each), scratch(2 * slots, each)],
        "chain", 9,
    )
    return corrected, residual


def solution(mesh):
    return jax.shard_map(
        body,
        mesh=mesh,
        in_specs=(
            P("space", None, None),
            P("tm", "space", None, None),
            P("space", None, None),
            P("space", None, None),
            P("tm"),
        ),
        out_specs=(P("tm", "space", None, None), P("tm", "space", None, None)),
        check_vma=False,
    )
```

```python
from functools import partial

import jax
import jax.numpy as jnp
import numpy as np
from jax import lax
from jax.experimental import pallas as pl
from jax.experimental.pallas import tpu as pltpu
from jax.sharding import PartitionSpec as P

COARSEN = 8
SWEEPS = 3
KAPPA_TOP = 3.0
SUB = 8
PLANES = 40
MATRIX = 3
VMEM = pltpu.CompilerParams(vmem_limit_bytes=48 * 2**20)


def polynomials(scale, top):
    middle = (top + 1.0) / 2.0
    spread = (top - 1.0) / 2.0
    relative = middle / spread

    def run(start, source):
        def apply(poly):
            return scale * np.concatenate([[0.0], poly])[: SWEEPS + 1]

        ratio_now = 1.0 / relative
        remain = source - apply(start)
        update = remain / middle
        iterate = start + update
        for _ in range(SWEEPS - 1):
            remain = remain - (update + apply(update))
            ratio_next = 1.0 / (2.0 * relative - ratio_now)
            update = ratio_next * ratio_now * update + (2.0 * ratio_next / spread) * remain
            iterate = iterate + update
            ratio_now = ratio_next
        return iterate

    one = np.zeros(SWEEPS + 1)
    one[0] = 1.0
    return run(one, 0.0 * one), run(0.0 * one, one)


def linear_factors(poly):
    roots = np.roots(poly[::-1] / poly[-1])
    assert np.all(np.abs(roots.imag) < 1e-9)
    return sorted((float(1.0 / r) for r in roots.real), reverse=True)


FINE_P, FINE_Q = polynomials(1.0, 1.0 + 12.0 * KAPPA_TOP)
COARSE_P, _ = polynomials(float(COARSEN), 1.0 + 12.0 * KAPPA_TOP * COARSEN)
FINE = linear_factors(FINE_P)
COARSE = linear_factors(COARSE_P)


def rows(ref, z, j, J):
    return ref[z, pl.ds(j, SUB, stride=J), :]


def put_rows(ref, z, j, J, value):
    ref[z, pl.ds(j, SUB, stride=J), :] = value


def copy_planes(n, dst, src, d0=0, s0=0):
    J = dst.shape[1]

    def one(z, c):
        for j in range(J):
            dst[d0 + z, j] = src[s0 + z, j]
        return c

    lax.fori_loop(0, n, one, 0, unroll=4 if n % 4 == 0 else 3 if n % 3 == 0 else 1)


def masks(width):
    lane = lax.broadcasted_iota(jnp.int32, (SUB, width), 1)
    sub = lax.broadcasted_iota(jnp.int32, (SUB, width), 0)
    return lane == 0, lane == width - 1, sub == 0, sub == SUB - 1


def lane_sums(parts, width):
    far = lax.broadcasted_iota(jnp.int32, (width, width), 0) - lax.broadcasted_iota(jnp.int32, (width, width), 1)
    ones = jnp.where(jnp.abs(far) == 1, 1.0, 0.0).astype(jnp.bfloat16)
    whole = jnp.concatenate(parts, axis=0)
    high = whole.astype(jnp.bfloat16)
    rest = whole - high.astype(jnp.float32)
    mid = rest.astype(jnp.bfloat16)
    low = (rest - mid.astype(jnp.float32)).astype(jnp.bfloat16)
    total = jnp.dot(
        jnp.concatenate([high, mid], axis=1), jnp.concatenate([ones, ones], axis=0), preferred_element_type=jnp.float32
    ) + jnp.dot(low, ones, preferred_element_type=jnp.float32)
    return [total[i * SUB : (i + 1) * SUB] for i in range(len(parts))]


def sweep(lo, hi, read, emit, J, width):
    first, last, top, bottom = masks(width)
    n = hi - lo
    steps = -(-n // PLANES)
    size = -(-n // steps)

    def chunk(i, c):
        z0 = jnp.minimum(lo + i * size, hi - size)
        planes = [[read(z0 + u, j) for j in range(J)] for u in range(size)]
        by_matrix = MATRIX if size >= 8 else 0
        if by_matrix:
            sums = lane_sums([w[j] for w in planes for j in range(J - by_matrix, J)], width)
        for u, w in enumerate(planes):
            z = z0 + u
            after = jnp.where(bottom, 0.0, pltpu.roll(w[0], SUB - 1, 0))
            before = jnp.where(top, 0.0, pltpu.roll(w[J - 1], 1, 0))
            for j in range(J):
                yp = w[j + 1] if j < J - 1 else after
                ym = w[j - 1] if j > 0 else before
                if j >= J - by_matrix:
                    xs = sums[u * by_matrix + j - (J - by_matrix)]
                else:
                    xs = jnp.where(first, 0.0, pltpu.roll(w[j], 1, 1)) + jnp.where(last, 0.0, pltpu.roll(w[j], width - 1, 1))
                beside = (read(z - 1, j) + read(z + 1, j)) + (yp + ym) + xs
                emit(z, j, w[j], beside)
        return c

    if steps == 1:
        chunk(0, 0)
    else:
        lax.fori_loop(0, steps, chunk, 0)


def factor(dst, src, cond, coef, lo, hi, s0=0, k0=0, extra=None):
    J, width = dst.shape[1], dst.shape[3]

    def emit(z, j, w, beside):
        out = w + (coef * cond[z + k0, j]) * (beside - 6.0 * w)
        if extra is not None:
            out = out + extra(z, j)
        dst[z, j] = out

    sweep(lo, hi, lambda z, j: src[z + s0, j], emit, J, width)


def fine_steps(a, b, cond, k0, total, levels, amounts=None, first_step=0, source=None):
    src, dst = a, b
    for level in range(levels):
        extra = None
        if source is not None and level % SWEEPS == SWEEPS - 1:
            amount = amounts[first_step + level // SWEEPS]
            extra = lambda z, j, amount=amount: amount * source[z + k0, j]
        factor(dst, src, cond, FINE[level % SWEEPS], level + 1, total - level - 1, k0=k0, extra=extra)
        src, dst = dst, src
    return src


def place_kernel(where, own, r1, r2, r3, field, field_up, field_dn, *, each):
    q = where[0]
    J = field.shape[1]
    for j, ref in enumerate((own, r1, r2, r3)):
        base = lax.bitwise_xor(q, j) * each
        for z in range(each):
            for row in range(J):
                field[base + z, row] = rows(ref, z, row, J)
    halo = field_up.shape[0]
    copy_planes(halo, field_up, field, 0, field.shape[0] - halo)
    copy_planes(halo, field_dn, field, 0, 0)


def coefficient_kernel(where, m0, m1, m2, m3, o0, o1, o2, o3, cond, force, raw, *, wide, halo, each):
    q, core = where[0], where[1]
    span, J, width = cond.shape[0], cond.shape[1], cond.shape[3]
    slab = span - 2 * wide
    skip = slab - wide
    for i, pieces in enumerate(zip((m0, m1, m2, m3), (o0, o1, o2, o3))):
        base = lax.bitwise_xor(q, i) * each
        for slot, ref in zip((core, 1 - core), pieces):
            for part in range(3):
                for z in range(each):
                    for j in range(J):
                        raw[slot, part * slab + base + z, j] = rows(ref, part * each + z, j, J)
    copy_planes(span, cond, raw.at[0], 0, skip)

    def inner(z, j, w, beside):
        raw[0, z + skip, j] = FINE_Q[1] * w + FINE_Q[2] * cond[z, j] * (6.0 * w - beside)

    def outer(z, j, w, beside):
        force[z, j] = FINE_Q[0] * raw[1, z + skip, j] + cond[z, j] * (6.0 * w - beside)

    margin = wide - (halo - SWEEPS)
    sweep(margin - 1, span - margin + 1, lambda z, j: raw[1, z + skip, j], inner, J, width)
    sweep(margin, span - margin, lambda z, j: raw[0, z + skip, j], outer, J, width)


def first_kernel(amounts, field, lo, hi, cond, force, out, up, dn, a, b, *, wide):
    slab, halo = field.shape[0], lo.shape[0]
    load_state(a, lo, field, hi)
    state = fine_steps(a, b, cond, wide - halo, slab + 2 * halo, halo, amounts, 0, force)
    copy_planes(slab, out, state, 0, halo)
    copy_planes(halo, up, state, 0, halo + slab - halo)
    copy_planes(halo, dn, state, 0, halo)


def load_state(a, lo, mid, hi):
    halo, slab = lo.shape[0], mid.shape[0]
    copy_planes(halo, a, lo, 0, 0)
    copy_planes(slab, a, mid, halo, 0)
    copy_planes(halo, a, hi, halo + slab, 0)


def second_kernel(
    where, amounts, field, lo, hi, cond, force, after,
    p0, p1, p2, p3, out, up, dn, a, b, *, wide, each, step,
):
    q = where[0]
    halo, slab, J = lo.shape[0], field.shape[0], a.shape[1]
    load_state(a, lo, field, hi)
    state = fine_steps(a, b, cond, wide - halo, slab + 2 * halo, halo, amounts, step, force)
    for i, piece in enumerate((p0, p1, p2, p3)):
        base = lax.bitwise_xor(q, i) * each
        for z in range(each):
            for j in range(J):
                value = state[halo + base + z, j]
                put_rows(piece, z, j, J, value)
                out[base + z, j] = value - after[base + z, j]
    copy_planes(halo, up, out, 0, slab - halo)
    copy_planes(halo, dn, out, 0, 0)


def third_kernel(field, lo, hi, cond, out, up, dn, a, b, *, wide):
    halo, slab = lo.shape[0], field.shape[0]
    load_state(a, lo, field, hi)
    state = fine_steps(a, b, cond, wide - halo, slab + 2 * halo, halo)
    copy_planes(slab, out, state, 0, halo)
    copy_planes(up.shape[0], up, state, 0, halo + slab - up.shape[0])
    copy_planes(dn.shape[0], dn, state, 0, halo)


def fourth_kernel(where, field, lo, hi, cond, out, p0, p1, p2, p3, a, b, *, levels, each):
    q = where[0]
    halo, slab, J = lo.shape[0], field.shape[0], a.shape[1]
    load_state(a, lo, field, hi)
    state = fine_steps(a, b, cond, 0, slab + 2 * halo, levels)
    copy_planes(out.shape[0], out, state, 0, levels)
    for i, piece in enumerate((p0, p1, p2, p3)):
        base = lax.bitwise_xor(q, i) * each
        for z in range(each):
            for j in range(J):
                put_rows(piece, z, j, J, state[halo + base + z, j])


def pair_kernel(where, mine, other, cond, out, both, a, b, *, wide):
    core = where[1]
    J = a.shape[1]
    total = mine.shape[0]
    slab = out.shape[0]

    def body(z, c):
        for j in range(J):
            both[core, z, j] = mine[z, j]
            both[1 - core, z, j] = other[z, j]
        return c

    lax.fori_loop(0, total, body, 0)
    k0 = wide - SWEEPS
    factor(a, both.at[0], cond, COARSE[0], 1, total - 1, k0=k0)
    factor(b, a, cond, COARSE[1], 2, total - 2, k0=k0)
    factor(a, b, cond, COARSE[2], 3, total - 3, k0=k0, extra=lambda z, j: both[1, z, j])
    half = out.shape[1]

    def give(z, c):
        for j in range(half):
            out[z, j] = a[SWEEPS + z, core * half + j]
        return c

    lax.fori_loop(0, slab, give, 0)


def order_kernel(where, own, r1, r2, r3, sums, send_up, send_dn, all_sums, *, reach):
    q = where[0]
    slab = own.shape[0]
    for i, ref in enumerate((own, r1, r2, r3)):
        copy_planes(slab, all_sums, ref, lax.bitwise_xor(q, i) * slab, 0)
    offset = 0
    for i, h in enumerate(reach):
        copy_planes(slab, sums, all_sums, i * slab, i * slab)
        copy_planes(h, send_up, all_sums, offset, (i + 1) * slab - h)
        copy_planes(h, send_dn, all_sums, offset, i * slab)
        offset += h


def chain_kernel(
    where, sums, got_lo, got_hi, other_sums, other_lo, other_hi, cond, *refs, wide, each, reach
):
    pieces, refs = refs[:10], refs[10:]
    corrected, residual, ends, a, b, c, d, relaxed, remain, error = refs
    q, core = where[0], where[1]
    J = a.shape[1]
    slab = sums.shape[0] // len(reach)
    half = J // 2
    mine_rel, other_rel, mine_res, other_res = pieces[:4], pieces[4], pieces[5:9], pieces[9]
    for i in range(4):
        place = lax.bitwise_xor(q, i)
        for z in range(each):
            for j in range(J):
                relaxed[2 * place + core, z, j] = rows(mine_rel[i], z, j, J)
                relaxed[2 * place + 1 - core, z, j] = rows(other_rel, i * each + z, j, J)
                remain[2 * place + 1 + core, z, j] = rows(mine_res[i], z, j, J)
                remain[2 * place + 2 - core, z, j] = rows(other_res, i * each + z, j, J)
    zero = jnp.zeros(a.shape[2:], jnp.float32)
    for z in range(each):
        for j in range(J):
            remain[0, z, j] = zero
            error[0, z, j] = zero
    offset = 0
    for i, h in enumerate(reach):

        def fill(n, mine, other, d0, s0, i=i):
            def one(z, carry):
                for j in range(half):
                    ends[i, d0 + z, core * half + j] = mine[s0 + z, j]
                    ends[i, d0 + z, (1 - core) * half + j] = other[s0 + z, j]
                return carry

            lax.fori_loop(0, n, one, 0)

        fill(h, got_lo, other_lo, 0, offset)
        fill(slab, sums, other_sums, h, i * slab)
        fill(h, got_hi, other_hi, h + slab, offset)
        offset += h
    top = reach[0]
    window = each + 2 * top
    base = each * q

    def keep(k, ref, s0):
        for z in range(each):
            for j in range(J):
                error[k, z, j] = ref[top + z + s0, j]

    keep(2, ends.at[0], base)
    for z in range(each):
        for j in range(J):
            error[1, z, j] = remain[1, z, j]
    src, s0, lo, hi = ends.at[0], base, 0, window
    for i in range(len(reach)):
        k = 2 * i + 3
        inner = dict(k0=base)
        m0, m1 = top, top + each
        factor(c, src, cond, COARSE[0], m0 - 2, m1 + 2, s0=s0, **inner)
        factor(d, c, cond, COARSE[1], m0 - 1, m1 + 1, **inner)
        factor(c, d, cond, COARSE[2], m0, m1, extra=lambda z, j, k=k: remain[k, z - top, j], **inner)
        keep(k, c, 0)
        if i + 1 < len(reach):
            nxt = ends.at[i + 1]
            shift = base - top + reach[i + 1]
            bufs = (a, b)
            for level in range(2 * SWEEPS):
                lo, hi = lo + 1, hi - 1
                dst = bufs[level % 2]
                extra = None
                if level == 2 * SWEEPS - 1:
                    extra = lambda z, j, nxt=nxt, shift=shift: nxt[z + shift, j]
                factor(dst, src, cond, COARSE[level % SWEEPS], lo, hi, s0=s0, extra=extra, **inner)
                src, s0 = dst, 0
            keep(2 * i + 4, src, 0)
    slots = corrected.shape[0]
    for i in range(slots):
        k = core * slots + i
        for z in range(each):
            for j in range(J):
                corrected[i, z, pl.ds(j, SUB, stride=J), :] = relaxed[k, z, j] + error[k, z, j]
                residual[i, z, pl.ds(j, SUB, stride=J), :] = remain[k, z, j]


def body(initial, guess, conduct, source, profile):
    slots, each, nx, ny = guess.shape
    J = nx // SUB
    cores = lax.axis_size("tm")
    count = lax.axis_size("space")
    assert cores == 2 and slots == 4 and count % slots == 0 and nx % SUB == 0
    core = lax.axis_index("tm")
    place = lax.axis_index("space")
    q = place % slots
    slab = slots * each
    halo = COARSEN * SWEEPS // 2
    wide = halo + SWEEPS
    where = jnp.stack([q, core]).astype(jnp.int32)
    f32 = jnp.float32

    def blocked(n):
        return jax.ShapeDtypeStruct((n, J, SUB, ny), f32)

    def natural(n):
        return jax.ShapeDtypeStruct((n, nx, ny), f32)

    def scratch(*lead):
        return pltpu.VMEM((*lead, J, SUB, ny), f32)

    smem = pl.BlockSpec(memory_space=pltpu.SMEM)
    vmem = pl.BlockSpec(memory_space=pltpu.VMEM)

    def call(kernel, scalars, arrays, outs, scratches, name, micros):
        return pl.pallas_call(
            kernel,
            out_shape=outs,
            in_specs=[smem] * len(scalars) + [vmem] * len(arrays),
            out_specs=jax.tree.map(lambda _: vmem, outs),
            scratch_shapes=scratches,
            compiler_params=VMEM,
            cost_estimate=pl.CostEstimate(
                flops=micros * 10**9, bytes_accessed=micros * 3 * 10**6, transcendentals=0
            ),
            name=name,
        )(*scalars, *arrays)

    def swap(value):
        return lax.ppermute(value, "tm", [(0, 1), (1, 0)])

    def across(value, j):
        return lax.ppermute(value, "space", [(s, s - s % slots + ((s % slots) ^ j)) for s in range(count)])

    def up(value):
        return lax.ppermute(value, "space", [(s, s + slots) for s in range(count - slots)])

    def down(value):
        return lax.ppermute(value, "space", [(s + slots, s) for s in range(count - slots)])

    first = core == 0
    theirs = swap(guess)
    low, high = jnp.where(first, guess, theirs), jnp.where(first, theirs, guess)
    guesses = jnp.concatenate([low, high], axis=0)
    amounts_other = swap(profile)
    profiles = jnp.concatenate([jnp.where(first, profile, amounts_other), jnp.where(first, amounts_other, profile)])
    task = 2 * q + core
    amounts = lax.dynamic_slice_in_dim(profiles, task * COARSEN, COARSEN)

    entries = jnp.concatenate([initial[None], guesses[:-1]], axis=0)
    coef = jnp.where(first, conduct, source)
    coef = jnp.concatenate([up(coef), coef, down(coef)], axis=0)

    def entry_for(j):
        return lax.dynamic_index_in_dim(entries, 2 * (q ^ j) + core, 0, False)

    def gathered(pieces):
        return [pieces[0]] + [across(pieces[j], j) for j in range(1, slots)]

    *entry, coef = lax.optimization_barrier((*gathered([entry_for(j) for j in range(slots)]), coef))
    field, send_up, send_dn = call(
        partial(place_kernel, each=each),
        [where], entry,
        [blocked(slab), blocked(halo), blocked(halo)], [], "place", 1,
    )
    mine = gathered([coef] * slots)
    lo, hi = up(send_up), down(send_dn)
    span, total = slab + 2 * wide, slab + 2 * halo
    others = [swap(m) for m in mine]
    cond, force = call(
        partial(coefficient_kernel, wide=wide, halo=halo, each=each),
        [where], [*mine, *others], [blocked(span), blocked(span)], [scratch(2, 3 * slab)], "coefficients", 4,
    )
    field_sent, lo = lax.optimization_barrier((field, lo))
    pairs = [(count + s, s) for s in range(count)] + [(s, count + s - 1) for s in range(count) if s % slots]
    after = lax.ppermute(field_sent, ("tm", "space"), pairs)
    state, send_up, send_dn = call(
        partial(first_kernel, wide=wide),
        [amounts], [field, lo, hi, cond, force],
        [blocked(slab), blocked(halo), blocked(halo)],
        [scratch(total), scratch(total)], "relax_first", 8,
    )
    after, send_up, send_dn = lax.optimization_barrier((after, send_up, send_dn))
    *rel, state, send_up, send_dn = call(
        partial(second_kernel, wide=wide, each=each, step=halo // SWEEPS),
        [where, amounts], [state, up(send_up), down(send_dn), cond, force, after],
        [natural(each)] * 4 + [blocked(slab), blocked(halo), blocked(halo)],
        [scratch(total), scratch(total)], "relax_second", 9,
    )
    lo, hi = up(send_up), down(send_dn)
    *rel, lo = lax.optimization_barrier((*rel, lo))
    rel = gathered(rel)
    state, send_up, send_dn = call(
        partial(third_kernel, wide=wide),
        [], [state, lo, hi, cond],
        [blocked(slab), blocked(wide), blocked(wide)],
        [scratch(total), scratch(total)], "again_first", 8,
    )
    *rel, send_up, send_dn = lax.optimization_barrier((*rel, send_up, send_dn))
    rel_other = swap(jnp.concatenate(rel, axis=0))
    lo, hi = up(send_up), down(send_dn)
    rel_other, lo = lax.optimization_barrier((rel_other, lo))
    remain, *res = call(
        partial(fourth_kernel, levels=halo, each=each),
        [where], [state, lo, hi, cond],
        [blocked(slab + 2 * SWEEPS)] + [natural(each)] * 4,
        [scratch(span), scratch(span)], "again_second", 9,
    )
    pair = call(
        partial(pair_kernel, wide=wide),
        [where], [remain, swap(remain), cond],
        jax.ShapeDtypeStruct((slab, J // 2, SUB, ny), f32),
        [scratch(2, slab + 2 * SWEEPS), scratch(slab + 2 * SWEEPS), scratch(slab + 2 * SWEEPS)], "pairs", 3,
    )
    reach = [2 * SWEEPS * (slots - 2 - i) + SWEEPS for i in range(slots - 1)]
    halves = lambda n: jax.ShapeDtypeStruct((n, J // 2, SUB, ny), f32)
    sums, send_up, send_dn = call(
        partial(order_kernel, reach=reach),
        [where], gathered([pair] * slots),
        [halves(len(reach) * slab), halves(sum(reach)), halves(sum(reach))],
        [pltpu.VMEM((slots * slab, J // 2, SUB, ny), f32)], "order", 1,
    )
    *res, sums = lax.optimization_barrier((*res, sums))
    res = gathered(res)
    res_other = swap(jnp.concatenate(res, axis=0))
    lo, hi = up(send_up), down(send_dn)
    window = each + 2 * reach[0]
    corrected, residual = call(
        partial(chain_kernel, wide=wide, each=each, reach=reach),
        [where], [sums, lo, hi, swap(sums), swap(lo), swap(hi), cond, *rel, rel_other, *res, res_other],
        [jax.ShapeDtypeStruct(guess.shape, f32)] * 2,
        [scratch(len(reach), slab + 2 * reach[0])]
        + [scratch(window)] * 4
        + [scratch(2 * slots, each), scratch(2 * slots + 1, each), scratch(2 * slots, each)],
        "chain", 9,
    )
    return corrected, residual


def solution(mesh):
    return jax.shard_map(
        body,
        mesh=mesh,
        in_specs=(
            P("space", None, None),
            P("tm", "space", None, None),
            P("space", None, None),
            P("space", None, None),
            P("tm"),
        ),
        out_specs=(P("tm", "space", None, None), P("tm", "space", None, None)),
        check_vma=False,
    )
```
